128 devices in a mesh: snap: 8 (over y_lo, z), rows: 16 (over y_hi, x, core).
Axes of the slice: x: 4, y: 4 (y_hi: 2, y_lo: 2; y = y_hi * 2 + y_lo), z: 4, core: 2. Of those that a mesh axis runs over, the one named last changes fastest.
Arguments:
- window_observations: bfloat16 [256, 2097152], P('snap', 'rows'), may hold values from -120 to 120
Outputs:
- transition_mapping: float32 [255, 255], replicated
- future_estimates: float32 [8, 2097152], P(None, ('rows', 'snap'))
The draws below stay inside these ranges and needn't reach their ends.
All inputs are finite; a program needn't handle non-finite values.
Results may differ from the reference program's by a relative error of at most 0.0003.
Values may be sent and summed in bfloat16 or wider, within the bound.
A program may use at most 128 MiB of HBM per device.

```python
import math
import jax
import jax.numpy as jnp
from jax import lax

S = 256
H = 8
CARD_ENTRY_COUNT = 16384
STATES = 2097152


def draw_window_observations(key, part):
    keys_all = jax.random.split(key, 5)
    mode_count = max(S // 16, 2)
    position = jnp.arange(STATES, dtype=jnp.float32) / STATES
    row_scale = jnp.exp(math.log(3.0) * position) * jnp.exp(jax.random.uniform(keys_all[4], (STATES,), jnp.float32, math.log(0.5), math.log(2.0)))
    noise = jax.random.truncated_normal(keys_all[0], -4.0, 4.0, (S, STATES), jnp.float32)
    amplitude = 0.5 * jax.random.truncated_normal(keys_all[1], -2.0, 2.0, (mode_count, STATES), jnp.float32)
    phases = jax.random.uniform(keys_all[2], (mode_count, STATES), jnp.float32, -math.pi, math.pi)
    frequency = jax.random.uniform(keys_all[3], (mode_count,), jnp.float32, 0.03, 3.0)
    moments = jnp.arange(S, dtype=jnp.float32)[:, None]

    def add_mode(mode_index, summed):
        return summed + amplitude[mode_index][None, :] * jnp.cos(frequency[mode_index] * moments + phases[mode_index][None, :])
    modal = lax.fori_loop(0, mode_count, add_mode, jnp.zeros((S, STATES), jnp.float32))
    return ((noise + modal) * row_scale[None, :]).astype(jnp.bfloat16)


def setup_inputs(seed: int = 0) -> dict:
    key_of = jax.random.split(jax.random.key(seed), 2)
    window_observations = draw_window_observations(jax.random.fold_in(key_of[1], 71), 0)
    return {"window_observations": window_observations}


exact_arithmetic = lax.Precision.HIGHEST

def upper_factor(matrix):
    return jnp.linalg.cholesky(matrix).T

def reference(window_observations):
    block_list = STATES // CARD_ENTRY_COUNT

    def add_block(block_index, summed):
        rows_here = lax.dynamic_slice_in_dim(window_observations, block_index * CARD_ENTRY_COUNT, CARD_ENTRY_COUNT, 1)
        return summed + jnp.dot(rows_here.astype(jnp.float32), rows_here.T.astype(jnp.float32), preferred_element_type=jnp.float32)
    gram_matrix = lax.fori_loop(0, block_list, add_block, jnp.zeros((S, S), jnp.float32))
    upper_full = upper_factor(gram_matrix)
    principal_section = S - 1
    upper_left_corner = upper_full[:principal_section, :principal_section]
    coords = upper_full[:principal_section, 1:]
    transition_mapping = jax.scipy.linalg.solve_triangular(upper_left_corner, coords.T, trans=1, lower=False).T
    vector = coords[:, principal_section - 1]
    columns = []
    for horizon in range(H):
        vector = jnp.dot(transition_mapping, vector, precision=exact_arithmetic)
        columns.append(vector)
    stacked = jnp.stack(columns, axis=1)
    combination_coefficient_arrays = jax.scipy.linalg.solve_triangular(upper_left_corner, stacked, lower=False)
    future_estimates = jnp.dot(combination_coefficient_arrays.T, window_observations[:principal_section].astype(jnp.float32), precision=exact_arithmetic)
    return (transition_mapping, future_estimates)
```

```python
import functools

import jax
import jax.numpy as jnp
from jax import lax
from jax.experimental import pallas as pl
from jax.experimental.pallas import tpu as pltpu
from jax.sharding import PartitionSpec as P

H = 8
BLOCK = 32
CHUNKS = 8
FORECAST_COLUMNS = 2048
MESH = pl.DeviceIdType.MESH
F32, BF16 = jnp.float32, jnp.bfloat16


def parts3(value):
    high = value.astype(BF16)
    rest = value - high.astype(F32)
    middle = rest.astype(BF16)
    low = (rest - middle.astype(F32)).astype(BF16)
    return high, middle, low


def exchange_kernel(n_snap, n_rows, x_ref, data_ref, gram_ref, held, total, slots, slab, laps,
                    own_sem, send_sem, recv_sem, out_sem, s1, r1, s2, r2, s3, r3):
    me_s, me_r = lax.axis_index("snap"), lax.axis_index("rows")
    block = x_ref.shape[0]
    states = data_ref.shape[1]
    width = states // CHUNKS
    share = gram_ref.shape[0] // n_rows

    def snap_peer(offset):
        return lax.rem(me_s + offset, n_snap)

    def rows_peer(offset):
        return lax.rem(me_r + offset, n_rows)

    barrier = pltpu.get_barrier_semaphore()
    for offset in range(1, n_snap):
        pl.semaphore_signal(barrier, inc=1, device_id=(snap_peer(offset), me_r), device_id_type=MESH)
    for offset in range(1, n_rows):
        pl.semaphore_signal(barrier, inc=1, device_id=(me_s, rows_peer(offset)), device_id_type=MESH)
    pl.semaphore_wait(barrier, n_snap + n_rows - 2)

    my_rows = pl.ds(pl.multiple_of(me_s * block, block), block)

    def columns(chunk):
        return pl.ds(pl.multiple_of(chunk * width, width), width)

    def own_copy(chunk):
        return pltpu.make_async_copy(
            x_ref.at[:, pl.ds(pl.multiple_of(me_s * states + chunk * width, width), width)],
            held.at[my_rows, columns(chunk)],
            own_sem.at[chunk],
        )

    def send(chunk, offset):
        peer = snap_peer(offset)
        return pltpu.make_async_remote_copy(
            src_ref=x_ref.at[:, pl.ds(pl.multiple_of(peer * states + chunk * width, width), width)],
            dst_ref=held.at[my_rows, columns(chunk)],
            send_sem=send_sem.at[chunk, offset],
            recv_sem=recv_sem.at[chunk, offset],
            device_id=(peer, me_r),
            device_id_type=MESH,
        )

    def start_chunk(chunk, carry):
        own_copy(chunk).start()
        for offset in range(1, n_snap):
            send(chunk, offset).start()
        return carry

    lax.fori_loop(0, CHUNKS, start_chunk, 0)
    total[...] = jnp.zeros_like(total)

    def out_copy(chunk):
        return pltpu.make_async_copy(held.at[:, columns(chunk)], data_ref.at[:, columns(chunk)], out_sem.at[chunk])

    def use_chunk(chunk, carry):
        own_copy(chunk).wait()
        for offset in range(1, n_snap):
            send(chunk, offset).wait_recv()
        out_copy(chunk).start()
        piece = held[:, columns(chunk)]
        total[...] += lax.dot_general(piece, piece, (((1,), (1,)), ((), ())), preferred_element_type=F32)
        return carry

    lax.fori_loop(0, CHUNKS, use_chunk, 0)

    def part_of(index):
        return pl.ds(pl.multiple_of(index * share, share), share)

    def first(offset):
        peer = rows_peer(offset)
        return pltpu.make_async_remote_copy(
            src_ref=total.at[part_of(peer)], dst_ref=slots.at[offset],
            send_sem=s1.at[offset], recv_sem=r1.at[offset],
            device_id=(me_s, peer), device_id_type=MESH,
        )

    for offset in range(1, n_rows):
        first(offset).start()
    mine = total[part_of(me_r)]
    for offset in range(1, n_rows):
        first(offset).wait_recv()
        mine = mine + slots[offset]
    slab[...] = mine

    def second(offset):
        return pltpu.make_async_remote_copy(
            src_ref=slab, dst_ref=laps.at[me_s],
            send_sem=s2.at[offset], recv_sem=r2.at[offset],
            device_id=(snap_peer(offset), me_r), device_id_type=MESH,
        )

    for offset in range(1, n_snap):
        second(offset).start()
    laps[me_s] = mine
    for offset in range(1, n_snap):
        second(offset).wait_recv()
    summed = laps[0]
    for index in range(1, n_snap):
        summed = summed + laps[index]
    gram_ref[part_of(me_r)] = summed

    def third(offset):
        return pltpu.make_async_remote_copy(
            src_ref=gram_ref.at[part_of(me_r)], dst_ref=gram_ref.at[part_of(me_r)],
            send_sem=s3.at[offset], recv_sem=r3.at[offset],
            device_id=(me_s, rows_peer(offset)), device_id_type=MESH,
        )

    for offset in range(1, n_rows):
        third(offset).start()
    for offset in range(1, n_rows):
        third(offset).wait_recv()
    for offset in range(1, n_rows):
        first(offset).wait_send()
        third(offset).wait_send()
    for offset in range(1, n_snap):
        second(offset).wait_send()

    def finish(chunk, carry):
        out_copy(chunk).wait()
        for offset in range(1, n_snap):
            send(chunk, offset).wait_send()
        return carry

    lax.fori_loop(0, CHUNKS, finish, 0)


def exchange(x, n_snap, n_rows):
    block, length = x.shape
    size, states = n_snap * block, length // n_snap
    share = size // n_rows
    dma = pltpu.SemaphoreType.DMA
    return pl.pallas_call(
        functools.partial(exchange_kernel, n_snap, n_rows),
        out_shape=(
            jax.ShapeDtypeStruct((size, states), BF16),
            jax.ShapeDtypeStruct((size, size), F32),
        ),
        in_specs=[pl.BlockSpec(memory_space=pltpu.HBM)],
        out_specs=(pl.BlockSpec(memory_space=pltpu.HBM), pl.BlockSpec(memory_space=pltpu.VMEM)),
        scratch_shapes=[
            pltpu.VMEM((size, states), BF16),
            pltpu.VMEM((size, size), F32),
            pltpu.VMEM((n_rows, share, size), F32),
            pltpu.VMEM((share, size), F32),
            pltpu.VMEM((n_snap, share, size), F32),
            dma((CHUNKS,)),
            dma((CHUNKS, n_snap)),
            dma((CHUNKS, n_snap)),
            dma((CHUNKS,)),
            dma((n_rows,)), dma((n_rows,)),
            dma((n_snap,)), dma((n_snap,)),
            dma((n_rows,)), dma((n_rows,)),
        ],
        compiler_params=pltpu.CompilerParams(
            collective_id=0, has_side_effects=True, vmem_limit_bytes=40 * 2**20
        ),
    )(x)


def factor_block(matrix):
    n = matrix.shape[0]
    rows = lax.broadcasted_iota(jnp.int32, (n, 128), 0)
    lanes = lax.broadcasted_iota(jnp.int32, (n, 128), 1)
    unit = jnp.where(lanes == rows + n, F32(1.0), F32(0.0))
    state = unit + jnp.concatenate([matrix, jnp.zeros((n, 128 - n), F32)], axis=1)
    for k in range(n - 1):
        column, row = state[:, k : k + 1], state[k : k + 1, :]
        inverse = F32(1.0) / state[k : k + 1, k : k + 1]
        state = state - (jnp.where(rows > k, column, F32(0.0)) * inverse) * row
    diagonal = jnp.sum(jnp.where(rows == lanes, state, F32(0.0)), axis=1, keepdims=True)
    return state, diagonal


def six_left(value, axis):
    high, middle, low = parts3(value)
    return jnp.concatenate([high, middle, high, low, high, middle], axis=axis)


def six_right(value, axis):
    high, middle, low = parts3(value)
    return jnp.concatenate([high, high, middle, high, low, middle], axis=axis)


def forecast_kernel(gram_ref, data_hbm, map_ref, future_ref, work, upper, lower, data, sems):
    size, states = data.shape
    pieces = sems.shape[0]
    width = states // pieces

    def fetch(index):
        part = pl.ds(index * width, width)
        return pltpu.make_async_copy(data_hbm.at[:, part], data.at[:, part], sems.at[index])

    for index in range(pieces):
        fetch(index).start()

    b = BLOCK
    work[...] = gram_ref[...]
    cols = lax.broadcasted_iota(jnp.int32, (b, size), 1)
    last = None
    for s in range(0, size, b):
        lines = work[s : s + b, :]
        state, diagonal = factor_block(lines[:, s : s + b])
        rows_b = lax.broadcasted_iota(jnp.int32, (b, size), 0)
        inside = (cols >= s) & (cols < s + b)
        lines = jnp.where(inside, jnp.where(cols == rows_b + s, F32(1.0), F32(0.0)), lines)
        solved = jnp.dot(
            six_left(state[:, b : 2 * b], 1), six_right(lines, 0), preferred_element_type=F32
        )
        if s + b < size:
            first = 0 if s + b < size // 2 else size // 2
            scaled = jnp.where(cols >= s + b, solved, F32(0.0)) * (F32(1.0) / diagonal)
            update = lax.dot_general(
                six_left(scaled[:, first:], 0), six_right(solved, 0), (((0,), (0,)), ((), ())),
                preferred_element_type=F32,
            )
            kept = work[s + b :, :]
            cols_k = lax.broadcasted_iota(jnp.int32, kept.shape, 1)
            kept = jnp.where((cols_k >= s) & (cols_k < s + b), F32(0.0), kept)
            work[s + b :, :] = kept - update[s + b - first :, :]
        root = lax.rsqrt(diagonal)
        corner = jnp.where(inside, F32(0.0), jnp.where(cols >= s + b, solved, F32(0.0)))
        placed = [state[:, :b]]
        if s:
            placed.insert(0, jnp.zeros((b, s), F32))
        if s + b < size:
            placed.append(jnp.zeros((b, size - s - b), F32))
        diag_rows = jnp.concatenate(placed, axis=1)
        diag_rows = jnp.where(cols >= rows_b + s, diag_rows, F32(0.0))
        upper[s : s + b, :] = (corner + diag_rows) * root
        low_rows = jnp.where(cols < s + b, solved, F32(0.0))
        lower[s : s + b, :] = low_rows * root
        last = low_rows

    cols_1 = lax.broadcasted_iota(jnp.int32, (1, size), 1)
    vector = jnp.where(cols_1 < size - 1, -last[b - 1 : b, :], F32(0.0))
    step, powers = vector, []
    for _ in range(H):
        moved = jnp.where((cols_1 >= 1) & (cols_1 < size - 1), pltpu.roll(step, 1, 1), F32(0.0))
        step = moved + vector * step[:, size - 2 : size - 1]
        powers.append(step)
    weights = jnp.concatenate(powers, axis=0)
    left = jnp.concatenate([part.astype(F32) for part in parts3(weights)], axis=0).astype(BF16)

    cols_w = lax.broadcasted_iota(jnp.int32, (size, size), 1)
    coords = jnp.where(cols_w < size - 1, pltpu.roll(upper[...], size - 1, 1), F32(0.0))
    mapping = lax.dot_general(
        coords, lower[...], (((1,), (1,)), ((), ())),
        precision=lax.Precision.HIGHEST, preferred_element_type=F32,
    )
    map_ref[...] = mapping[: size - 1, : size - 1]

    for index in range(pieces):
        fetch(index).wait()
        part = pl.ds(index * width, width)
        product = jnp.dot(left, data[:, part], preferred_element_type=F32)
        future_ref[:, part] = product[:H] + product[H : 2 * H] + product[2 * H :]


def forecast(gram, data):
    size, states = data.shape
    return pl.pallas_call(
        forecast_kernel,
        out_shape=(
            jax.ShapeDtypeStruct((size - 1, size - 1), F32),
            jax.ShapeDtypeStruct((H, states), F32),
        ),
        in_specs=[pl.BlockSpec(memory_space=pltpu.VMEM), pl.BlockSpec(memory_space=pltpu.HBM)],
        out_specs=(pl.BlockSpec(memory_space=pltpu.VMEM), pl.BlockSpec(memory_space=pltpu.VMEM)),
        scratch_shapes=[
            pltpu.VMEM((size, size), F32),
            pltpu.VMEM((size, size), F32),
            pltpu.VMEM((size, size), F32),
            pltpu.VMEM((size, states), BF16),
            pltpu.SemaphoreType.DMA((states // FORECAST_COLUMNS,)),
        ],
        compiler_params=pltpu.CompilerParams(vmem_limit_bytes=40 * 2**20),
    )(gram, data)


def solution(mesh):
    n_snap, n_rows = mesh.shape["snap"], mesh.shape["rows"]

    def per_device(window_observations):
        data, gram = exchange(window_observations, n_snap, n_rows)
        return forecast(gram, data)

    return jax.shard_map(
        per_device,
        mesh=mesh,
        in_specs=(P("snap", "rows"),),
        out_specs=(P(), P(None, ("rows", "snap"))),
        check_vma=False,
    )
```

```python
import functools

import jax
import jax.numpy as jnp
from jax import lax
from jax.experimental import pallas as pl
from jax.experimental.pallas import tpu as pltpu
from jax.sharding import PartitionSpec as P

H = 8
BLOCK = 32
CHUNKS = 8
FORECAST_COLUMNS = 2048
MESH = pl.DeviceIdType.MESH
F32, BF16 = jnp.float32, jnp.bfloat16


def parts3(value):
    high = value.astype(BF16)
    rest = value - high.astype(F32)
    middle = rest.astype(BF16)
    low = (rest - middle.astype(F32)).astype(BF16)
    return high, middle, low


def exchange_kernel(n_snap, n_rows, x_ref, data_ref, gram_ref, held, total, slots, slab, laps,
                    own_sem, send_sem, recv_sem, out_sem, s1, r1, s2, r2, s3, r3):
    me_s, me_r = lax.axis_index("snap"), lax.axis_index("rows")
    block = x_ref.shape[0]
    states = data_ref.shape[1]
    width = states // CHUNKS
    share = gram_ref.shape[0] // n_rows

    def snap_peer(offset):
        return lax.rem(me_s + offset, n_snap)

    def rows_peer(offset):
        return lax.rem(me_r + offset, n_rows)

    barrier = pltpu.get_barrier_semaphore()
    for offset in range(1, n_snap):
        pl.semaphore_signal(barrier, inc=1, device_id=(snap_peer(offset), me_r), device_id_type=MESH)
    for offset in range(1, n_rows):
        pl.semaphore_signal(barrier, inc=1, device_id=(me_s, rows_peer(offset)), device_id_type=MESH)
    pl.semaphore_wait(barrier, n_snap + n_rows - 2)

    my_rows = pl.ds(pl.multiple_of(me_s * block, block), block)

    def columns(chunk):
        return pl.ds(pl.multiple_of(chunk * width, width), width)

    def own_copy(chunk):
        return pltpu.make_async_copy(
            x_ref.at[:, pl.ds(pl.multiple_of(me_s * states + chunk * width, width), width)],
            held.at[my_rows, columns(chunk)],
            own_sem.at[chunk],
        )

    def send(chunk, offset):
        peer = snap_peer(offset)
        return pltpu.make_async_remote_copy(
            src_ref=x_ref.at[:, pl.ds(pl.multiple_of(peer * states + chunk * width, width), width)],
            dst_ref=held.at[my_rows, columns(chunk)],
            send_sem=send_sem.at[chunk, offset],
            recv_sem=recv_sem.at[chunk, offset],
            device_id=(peer, me_r),
            device_id_type=MESH,
        )

    def start_chunk(chunk, carry):
        own_copy(chunk).start()
        for offset in range(1, n_snap):
            send(chunk, offset).start()
        return carry

    lax.fori_loop(0, CHUNKS, start_chunk, 0)
    total[...] = jnp.zeros_like(total)

    def out_copy(chunk):
        return pltpu.make_async_copy(held.at[:, columns(chunk)], data_ref.at[:, columns(chunk)], out_sem.at[chunk])

    def use_chunk(chunk, carry):
        own_copy(chunk).wait()
        for offset in range(1, n_snap):
            send(chunk, offset).wait_recv()
        out_copy(chunk).start()
        piece = held[:, columns(chunk)]
        total[...] += lax.dot_general(piece, piece, (((1,), (1,)), ((), ())), preferred_element_type=F32)
        return carry

    lax.fori_loop(0, CHUNKS, use_chunk, 0)

    def part_of(index):
        return pl.ds(pl.multiple_of(index * share, share), share)

    def first(offset):
        peer = rows_peer(offset)
        return pltpu.make_async_remote_copy(
            src_ref=total.at[part_of(peer)], dst_ref=slots.at[offset],
            send_sem=s1.at[offset], recv_sem=r1.at[offset],
            device_id=(me_s, peer), device_id_type=MESH,
        )

    for offset in range(1, n_rows):
        first(offset).start()
    mine = total[part_of(me_r)]
    for offset in range(1, n_rows):
        first(offset).wait_recv()
        mine = mine + slots[offset]
    slab[...] = mine

    def second(offset):
        return pltpu.make_async_remote_copy(
            src_ref=slab, dst_ref=laps.at[me_s],
            send_sem=s2.at[offset], recv_sem=r2.at[offset],
            device_id=(snap_peer(offset), me_r), device_id_type=MESH,
        )

    for offset in range(1, n_snap):
        second(offset).start()
    laps[me_s] = mine
    for offset in range(1, n_snap):
        second(offset).wait_recv()
    summed = laps[0]
    for index in range(1, n_snap):
        summed = summed + laps[index]
    gram_ref[part_of(me_r)] = summed

    def third(offset):
        return pltpu.make_async_remote_copy(
            src_ref=gram_ref.at[part_of(me_r)], dst_ref=gram_ref.at[part_of(me_r)],
            send_sem=s3.at[offset], recv_sem=r3.at[offset],
            device_id=(me_s, rows_peer(offset)), device_id_type=MESH,
        )

    for offset in range(1, n_rows):
        third(offset).start()
    for offset in range(1, n_rows):
        third(offset).wait_recv()
    for offset in range(1, n_rows):
        first(offset).wait_send()
        third(offset).wait_send()
    for offset in range(1, n_snap):
        second(offset).wait_send()

    def finish(chunk, carry):
        out_copy(chunk).wait()
        for offset in range(1, n_snap):
            send(chunk, offset).wait_send()
        return carry

    lax.fori_loop(0, CHUNKS, finish, 0)


def exchange(x, n_snap, n_rows):
    block, length = x.shape
    size, states = n_snap * block, length // n_snap
    share = size // n_rows
    dma = pltpu.SemaphoreType.DMA
    return pl.pallas_call(
        functools.partial(exchange_kernel, n_snap, n_rows),
        out_shape=(
            jax.ShapeDtypeStruct((size, states), BF16),
            jax.ShapeDtypeStruct((size, size), F32),
        ),
        in_specs=[pl.BlockSpec(memory_space=pltpu.HBM)],
        out_specs=(pl.BlockSpec(memory_space=pltpu.HBM), pl.BlockSpec(memory_space=pltpu.VMEM)),
        scratch_shapes=[
            pltpu.VMEM((size, states), BF16),
            pltpu.VMEM((size, size), F32),
            pltpu.VMEM((n_rows, share, size), F32),
            pltpu.VMEM((share, size), F32),
            pltpu.VMEM((n_snap, share, size), F32),
            dma((CHUNKS,)),
            dma((CHUNKS, n_snap)),
            dma((CHUNKS, n_snap)),
            dma((CHUNKS,)),
            dma((n_rows,)), dma((n_rows,)),
            dma((n_snap,)), dma((n_snap,)),
            dma((n_rows,)), dma((n_rows,)),
        ],
        compiler_params=pltpu.CompilerParams(
            collective_id=0, has_side_effects=True, vmem_limit_bytes=40 * 2**20
        ),
    )(x)


def reciprocal(value):
    guess = pltpu.reciprocal(value, approx=True)
    for _ in range(2):
        guess = guess * (F32(2.0) - value * guess)
    return guess


def factor_block(matrix):
    n = matrix.shape[0]
    rows = lax.broadcasted_iota(jnp.int32, (n, 128), 0)
    lanes = lax.broadcasted_iota(jnp.int32, (n, 128), 1)
    unit = jnp.where(lanes == rows + n, F32(1.0), F32(0.0))
    whole = unit + jnp.concatenate([matrix, jnp.zeros((n, 128 - n), F32)], axis=1)
    eight = lax.broadcasted_iota(jnp.int32, (8, 128), 0)
    tiles = [whole[k : k + 8] for k in range(0, n, 8)]

    def spread(tile, lane):
        return jnp.broadcast_to(tile[:, lane : lane + 1], (8, 128))

    for now, tile in enumerate(tiles):
        k = 8 * now
        later = range(now + 1, len(tiles))
        row = [jnp.broadcast_to(tile[i : i + 1], (8, 128)) for i in range(8)]
        column = {t: [spread(tiles[t], k + i) for i in range(8)] for t in later}
        pivot = [[spread(row[i], k + j) if j >= i else None for j in range(8)] for i in range(8)]
        inverse = [None] * 8
        for i in range(8):
            if i == 7 and not later:
                break
            inverse[i] = reciprocal(pivot[i][i])
            for j in range(i + 1, 8):
                factor = pivot[i][j] * inverse[i]
                for m in range(j, 8):
                    pivot[j][m] = pivot[j][m] - factor * pivot[i][m]
                row[j] = row[j] - factor * row[i]
                for t in later:
                    column[t][j] = column[t][j] - column[t][i] * factor
        for t in later:
            for i in range(8):
                tiles[t] = tiles[t] - (column[t][i] * inverse[i]) * row[i]
        done = row[0]
        for i in range(1, 8):
            done = jnp.where(eight == i, row[i], done)
        tiles[now] = done
    state = jnp.concatenate(tiles, axis=0)
    diagonal = jnp.sum(jnp.where(rows == lanes, state, F32(0.0)), axis=1, keepdims=True)
    return state, diagonal


def six_left(value, axis):
    high, middle, low = parts3(value)
    return jnp.concatenate([high, middle, high, low, high, middle], axis=axis)


def six_right(value, axis):
    high, middle, low = parts3(value)
    return jnp.concatenate([high, high, middle, high, low, middle], axis=axis)


def forecast_kernel(gram_ref, data_hbm, map_ref, future_ref, work, upper, lower, data, sems):
    size, states = data.shape
    pieces = sems.shape[0]
    width = states // pieces

    def fetch(index):
        part = pl.ds(index * width, width)
        return pltpu.make_async_copy(data_hbm.at[:, part], data.at[:, part], sems.at[index])

    for index in range(pieces):
        fetch(index).start()

    b = BLOCK
    work[...] = gram_ref[...]
    cols = lax.broadcasted_iota(jnp.int32, (b, size), 1)
    last = None
    for s in range(0, size, b):
        lines = work[s : s + b, :]
        state, diagonal = factor_block(lines[:, s : s + b])
        rows_b = lax.broadcasted_iota(jnp.int32, (b, size), 0)
        inside = (cols >= s) & (cols < s + b)
        lines = jnp.where(inside, jnp.where(cols == rows_b + s, F32(1.0), F32(0.0)), lines)
        solved = jnp.dot(
            six_left(state[:, b : 2 * b], 1), six_right(lines, 0), preferred_element_type=F32
        )
        if s + b < size:
            first = 0 if s + b < size // 2 else size // 2
            scaled = jnp.where(cols >= s + b, solved, F32(0.0)) * (F32(1.0) / diagonal)
            update = lax.dot_general(
                six_left(scaled[:, first:], 0), six_right(solved, 0), (((0,), (0,)), ((), ())),
                preferred_element_type=F32,
            )
            kept = work[s + b :, :]
            cols_k = lax.broadcasted_iota(jnp.int32, kept.shape, 1)
            kept = jnp.where((cols_k >= s) & (cols_k < s + b), F32(0.0), kept)
            work[s + b :, :] = kept - update[s + b - first :, :]
        root = lax.rsqrt(diagonal)
        corner = jnp.where(inside, F32(0.0), jnp.where(cols >= s + b, solved, F32(0.0)))
        placed = [state[:, :b]]
        if s:
            placed.insert(0, jnp.zeros((b, s), F32))
        if s + b < size:
            placed.append(jnp.zeros((b, size - s - b), F32))
        diag_rows = jnp.concatenate(placed, axis=1)
        diag_rows = jnp.where(cols >= rows_b + s, diag_rows, F32(0.0))
        upper[s : s + b, :] = (corner + diag_rows) * root
        low_rows = jnp.where(cols < s + b, solved, F32(0.0))
        lower[s : s + b, :] = low_rows * root
        last = low_rows

    cols_1 = lax.broadcasted_iota(jnp.int32, (1, size), 1)
    vector = jnp.where(cols_1 < size - 1, -last[b - 1 : b, :], F32(0.0))
    step, powers = vector, []
    for _ in range(H):
        moved = jnp.where((cols_1 >= 1) & (cols_1 < size - 1), pltpu.roll(step, 1, 1), F32(0.0))
        step = moved + vector * step[:, size - 2 : size - 1]
        powers.append(step)
    weights = jnp.concatenate(powers, axis=0)
    left = jnp.concatenate([part.astype(F32) for part in parts3(weights)], axis=0).astype(BF16)

    cols_w = lax.broadcasted_iota(jnp.int32, (size, size), 1)
    coords = jnp.where(cols_w < size - 1, pltpu.roll(upper[...], size - 1, 1), F32(0.0))
    mapping = lax.dot_general(
        coords, lower[...], (((1,), (1,)), ((), ())),
        precision=lax.Precision.HIGHEST, preferred_element_type=F32,
    )
    map_ref[...] = mapping[: size - 1, : size - 1]

    for index in range(pieces):
        fetch(index).wait()
        part = pl.ds(index * width, width)
        product = jnp.dot(left, data[:, part], preferred_element_type=F32)
        future_ref[:, part] = product[:H] + product[H : 2 * H] + product[2 * H :]


def forecast(gram, data):
    size, states = data.shape
    return pl.pallas_call(
        forecast_kernel,
        out_shape=(
            jax.ShapeDtypeStruct((size - 1, size - 1), F32),
            jax.ShapeDtypeStruct((H, states), F32),
        ),
        in_specs=[pl.BlockSpec(memory_space=pltpu.VMEM), pl.BlockSpec(memory_space=pltpu.HBM)],
        out_specs=(pl.BlockSpec(memory_space=pltpu.VMEM), pl.BlockSpec(memory_space=pltpu.VMEM)),
        scratch_shapes=[
            pltpu.VMEM((size, size), F32),
            pltpu.VMEM((size, size), F32),
            pltpu.VMEM((size, size), F32),
            pltpu.VMEM((size, states), BF16),
            pltpu.SemaphoreType.DMA((states // FORECAST_COLUMNS,)),
        ],
        compiler_params=pltpu.CompilerParams(vmem_limit_bytes=40 * 2**20),
    )(gram, data)


def solution(mesh):
    n_snap, n_rows = mesh.shape["snap"], mesh.shape["rows"]

    def per_device(window_observations):
        data, gram = exchange(window_observations, n_snap, n_rows)
        return forecast(gram, data)

    return jax.shard_map(
        per_device,
        mesh=mesh,
        in_specs=(P("snap", "rows"),),
        out_specs=(P(), P(None, ("rows", "snap"))),
        check_vma=False,
    )
```

```python
import functools

import jax
import jax.numpy as jnp
from jax import lax
from jax.experimental import pallas as pl
from jax.experimental.pallas import tpu as pltpu
from jax.sharding import PartitionSpec as P

H = 8
BLOCK = 32
CHUNKS = 8
EARLY = 3
SIDE = 4
FORECAST_COLUMNS = 2048
MESH = pl.DeviceIdType.MESH
F32, BF16 = jnp.float32, jnp.bfloat16


def parts3(value):
    high = value.astype(BF16)
    rest = value - high.astype(F32)
    middle = rest.astype(BF16)
    low = (rest - middle.astype(F32)).astype(BF16)
    return high, middle, low


def exchange_kernel(x_ref, data_ref, gram_ref, held, total, pair, quarters, slab, laps,
                    near_sem, own_sem, send_sem, recv_sem, out_sem, sum_send, sum_recv):
    me_s, me_r = lax.axis_index("snap"), lax.axis_index("rows")
    y_lo, z = me_s // SIDE, lax.rem(me_s, SIDE)
    y_hi, x, core = me_r // (2 * SIDE), lax.rem(me_r // 2, SIDE), lax.rem(me_r, 2)
    y = 2 * y_hi + y_lo
    block = x_ref.shape[0]
    states = data_ref.shape[1]
    width = states // CHUNKS

    def device(dx=0, dy=0, dz=0, dc=0):
        far_y = lax.rem(y + dy, SIDE)
        far_x, far_z, far_c = lax.rem(x + dx, SIDE), lax.rem(z + dz, SIDE), lax.rem(core + dc, 2)
        return (lax.rem(far_y, 2) * SIDE + far_z, (far_y // 2) * 2 * SIDE + far_x * 2 + far_c)

    neighbours = [
        device(dc=1), device(dx=1), device(dx=3), device(dy=1), device(dy=3), device(dz=1), device(dz=3)
    ]

    def greet(semaphore):
        for neighbour in neighbours:
            pl.semaphore_signal(semaphore, inc=1, device_id=neighbour, device_id_type=MESH)
        pl.semaphore_wait(semaphore, len(neighbours))

    my_rows = pl.ds(pl.multiple_of(me_s * block, block), block)

    def columns(chunk):
        return pl.ds(pl.multiple_of(chunk * width, width), width)

    def own_copy(chunk):
        return pltpu.make_async_copy(
            x_ref.at[:, pl.ds(pl.multiple_of(me_s * states + chunk * width, width), width)],
            held.at[my_rows, columns(chunk)],
            own_sem.at[chunk],
        )

    def send(chunk, offset):
        dy, dz = offset // SIDE, offset % SIDE
        peer = lax.rem(y_lo + dy, 2) * SIDE + lax.rem(z + dz, SIDE)
        return pltpu.make_async_remote_copy(
            src_ref=x_ref.at[:, pl.ds(pl.multiple_of(peer * states + chunk * width, width), width)],
            dst_ref=held.at[my_rows, columns(chunk)],
            send_sem=send_sem.at[chunk, offset],
            recv_sem=recv_sem.at[chunk, offset],
            device_id=(peer, me_r),
            device_id_type=MESH,
        )

    others = range(1, 2 * SIDE)

    def start_chunks(first, last, offsets):
        def start(chunk, carry):
            for offset in offsets:
                send(chunk, offset).start()
            return carry

        lax.fori_loop(first, last, start, 0)

    greet(pltpu.get_barrier_semaphore())
    start_chunks(0, EARLY, (4, 1, 3))
    greet(near_sem.at[0])
    start_chunks(0, EARLY, (2, 5, 7))
    greet(near_sem.at[1])
    start_chunks(0, EARLY, (6,))
    start_chunks(EARLY, CHUNKS, (6, 5, 7, 2, 4, 1, 3))
    greet(near_sem.at[2])

    def start_own(chunk, carry):
        own_copy(chunk).start()
        return carry

    lax.fori_loop(0, CHUNKS, start_own, 0)
    total[...] = jnp.zeros_like(total)

    def out_copy(chunk):
        return pltpu.make_async_copy(held.at[:, columns(chunk)], data_ref.at[:, columns(chunk)], out_sem.at[chunk])

    def use_chunk(chunk, carry):
        own_copy(chunk).wait()
        for offset in others:
            send(chunk, offset).wait_recv()
        out_copy(chunk).start()
        piece = held[:, columns(chunk)]
        half = piece.shape[0] // 2
        dims = (((1,), (1,)), ((), ()))
        top = lax.dot_general(piece[:half], piece, dims, preferred_element_type=F32)
        total[:half] += top[:, :half]
        total[half : 2 * half] += top[:, half:]
        total[2 * half :] += lax.dot_general(piece[half:], piece[half:], dims, preferred_element_type=F32)
        return carry

    lax.fori_loop(0, CHUNKS, use_chunk, 0)

    height = total.shape[0]
    half, share = height // 2, height // (2 * SIDE)
    started = []

    def move(source, target, where):
        index = len(started)
        copy = pltpu.make_async_remote_copy(
            src_ref=source, dst_ref=target, send_sem=sum_send.at[index], recv_sem=sum_recv.at[index],
            device_id=where, device_id_type=MESH,
        )
        copy.start()
        started.append(copy)
        return copy

    def half_of(index):
        return pl.ds(pl.multiple_of(index * half, half), half)

    def share_of(far_x):
        return pl.ds(pl.multiple_of(core * half + far_x * share, share), share)

    move(total.at[half_of(1 - core)], pair, device(dc=1)).wait_recv()
    pair[...] = pair[...] + total[half_of(core)]

    copies = []
    for dx in (2, 1, 3):
        part = pl.ds(pl.multiple_of(lax.rem(x + dx, SIDE) * share, share), share)
        copies.append(move(pair.at[part], quarters.at[dx], device(dx=dx)))
    mine = pair[pl.ds(pl.multiple_of(x * share, share), share)]
    for dx, copy in zip((2, 1, 3), copies):
        copy.wait_recv()
        mine = mine + quarters[dx]
    slab[...] = mine

    place = y * SIDE + z
    copies = []
    for dy in (2, 1, 3, 0):
        for dz in (2, 1, 3, 0):
            if dy or dz:
                copies.append(move(slab, laps.at[place], device(dy=dy, dz=dz)))
    laps[place] = mine
    for copy in copies:
        copy.wait_recv()
    summed = laps[0]
    for index in range(1, SIDE * SIDE):
        summed = summed + laps[index]
    gram_ref[share_of(x)] = summed

    copies = []
    for dx in (2, 1, 3):
        copies.append(move(gram_ref.at[share_of(x)], gram_ref.at[share_of(x)], device(dx=dx)))
    for copy in copies:
        copy.wait_recv()
    move(gram_ref.at[half_of(core)], gram_ref.at[half_of(core)], device(dc=1)).wait_recv()
    for copy in started:
        copy.wait_send()

    def finish(chunk, carry):
        out_copy(chunk).wait()
        for offset in others:
            send(chunk, offset).wait_send()
        return carry

    lax.fori_loop(0, CHUNKS, finish, 0)


def exchange(x):
    block, length = x.shape
    size, states = 2 * SIDE * block, length // (2 * SIDE)
    height, lanes = 3 * size // 2, size // 2
    share = height // (2 * SIDE)
    dma = pltpu.SemaphoreType.DMA
    moves = 2 + 2 * (SIDE - 1) + SIDE * SIDE - 1
    return pl.pallas_call(
        exchange_kernel,
        out_shape=(
            jax.ShapeDtypeStruct((size, states), BF16),
            jax.ShapeDtypeStruct((height, lanes), F32),
        ),
        in_specs=[pl.BlockSpec(memory_space=pltpu.HBM)],
        out_specs=(pl.BlockSpec(memory_space=pltpu.HBM), pl.BlockSpec(memory_space=pltpu.VMEM)),
        scratch_shapes=[
            pltpu.VMEM((size, states), BF16),
            pltpu.VMEM((height, lanes), F32),
            pltpu.VMEM((height // 2, lanes), F32),
            pltpu.VMEM((SIDE, share, lanes), F32),
            pltpu.VMEM((share, lanes), F32),
            pltpu.VMEM((SIDE * SIDE, share, lanes), F32),
            pltpu.SemaphoreType.REGULAR((3,)),
            dma((CHUNKS,)),
            dma((CHUNKS, 2 * SIDE)),
            dma((CHUNKS, 2 * SIDE)),
            dma((CHUNKS,)),
            dma((moves,)),
            dma((moves,)),
        ],
        compiler_params=pltpu.CompilerParams(
            collective_id=0, has_side_effects=True, vmem_limit_bytes=40 * 2**20
        ),
    )(x)


def reciprocal(value):
    guess = pltpu.reciprocal(value, approx=True)
    for _ in range(2):
        guess = guess * (F32(2.0) - value * guess)
    return guess


def factor_block(matrix):
    n = matrix.shape[0]
    rows = lax.broadcasted_iota(jnp.int32, (n, 128), 0)
    lanes = lax.broadcasted_iota(jnp.int32, (n, 128), 1)
    unit = jnp.where(lanes == rows + n, F32(1.0), F32(0.0))
    whole = unit + jnp.concatenate([matrix, jnp.zeros((n, 128 - n), F32)], axis=1)
    eight = lax.broadcasted_iota(jnp.int32, (8, 128), 0)
    tiles = [whole[k : k + 8] for k in range(0, n, 8)]

    def spread(tile, lane):
        return jnp.broadcast_to(tile[:, lane : lane + 1], (8, 128))

    for now, tile in enumerate(tiles):
        k = 8 * now
        later = range(now + 1, len(tiles))
        row = [jnp.broadcast_to(tile[i : i + 1], (8, 128)) for i in range(8)]
        column = {t: [spread(tiles[t], k + i) for i in range(8)] for t in later}
        pivot = [[spread(row[i], k + j) if j >= i else None for j in range(8)] for i in range(8)]
        inverse = [None] * 8
        for i in range(8):
            if i == 7 and not later:
                break
            inverse[i] = reciprocal(pivot[i][i])
            for j in range(i + 1, 8):
                factor = pivot[i][j] * inverse[i]
                for m in range(j, 8):
                    pivot[j][m] = pivot[j][m] - factor * pivot[i][m]
                row[j] = row[j] - factor * row[i]
                for t in later:
                    column[t][j] = column[t][j] - column[t][i] * factor
        for t in later:
            for i in range(8):
                tiles[t] = tiles[t] - (column[t][i] * inverse[i]) * row[i]
        done = row[0]
        for i in range(1, 8):
            done = jnp.where(eight == i, row[i], done)
        tiles[now] = done
    state = jnp.concatenate(tiles, axis=0)
    diagonal = jnp.sum(jnp.where(rows == lanes, state, F32(0.0)), axis=1, keepdims=True)
    return state, diagonal


def six_left(value, axis):
    high, middle, low = parts3(value)
    return jnp.concatenate([high, middle, high, low, high, middle], axis=axis)


def six_right(value, axis):
    high, middle, low = parts3(value)
    return jnp.concatenate([high, high, middle, high, low, middle], axis=axis)


def forecast_kernel(gram_ref, data_hbm, map_ref, future_ref, work, upper, lower, data, sems):
    size, states = data.shape
    pieces = sems.shape[0]
    width = states // pieces

    def fetch(index):
        part = pl.ds(index * width, width)
        return pltpu.make_async_copy(data_hbm.at[:, part], data.at[:, part], sems.at[index])

    for index in range(pieces):
        fetch(index).start()

    b = BLOCK
    half = size // 2
    work[:half, :half] = gram_ref[:half]
    work[:half, half:] = gram_ref[half : 2 * half]
    work[half:, half:] = gram_ref[2 * half :]
    work[half:, :half] = jnp.zeros((half, half), F32)
    cols = lax.broadcasted_iota(jnp.int32, (b, size), 1)
    last = None
    for s in range(0, size, b):
        lines = work[s : s + b, :]
        state, diagonal = factor_block(lines[:, s : s + b])
        rows_b = lax.broadcasted_iota(jnp.int32, (b, size), 0)
        inside = (cols >= s) & (cols < s + b)
        lines = jnp.where(inside, jnp.where(cols == rows_b + s, F32(1.0), F32(0.0)), lines)
        solved = jnp.dot(
            six_left(state[:, b : 2 * b], 1), six_right(lines, 0), preferred_element_type=F32
        )
        if s + b < size:
            first = 0 if s + b < size // 2 else size // 2
            scaled = jnp.where(cols >= s + b, solved, F32(0.0)) * (F32(1.0) / diagonal)
            update = lax.dot_general(
                six_left(scaled[:, first:], 0), six_right(solved, 0), (((0,), (0,)), ((), ())),
                preferred_element_type=F32,
            )
            kept = work[s + b :, :]
            cols_k = lax.broadcasted_iota(jnp.int32, kept.shape, 1)
            kept = jnp.where((cols_k >= s) & (cols_k < s + b), F32(0.0), kept)
            work[s + b :, :] = kept - update[s + b - first :, :]
        root = lax.rsqrt(diagonal)
        corner = jnp.where(inside, F32(0.0), jnp.where(cols >= s + b, solved, F32(0.0)))
        placed = [state[:, :b]]
        if s:
            placed.insert(0, jnp.zeros((b, s), F32))
        if s + b < size:
            placed.append(jnp.zeros((b, size - s - b), F32))
        diag_rows = jnp.concatenate(placed, axis=1)
        diag_rows = jnp.where(cols >= rows_b + s, diag_rows, F32(0.0))
        upper[s : s + b, :] = (corner + diag_rows) * root
        low_rows = jnp.where(cols < s + b, solved, F32(0.0))
        lower[s : s + b, :] = low_rows * root
        last = low_rows

    cols_1 = lax.broadcasted_iota(jnp.int32, (1, size), 1)
    vector = jnp.where(cols_1 < size - 1, -last[b - 1 : b, :], F32(0.0))
    step, powers = vector, []
    for _ in range(H):
        moved = jnp.where((cols_1 >= 1) & (cols_1 < size - 1), pltpu.roll(step, 1, 1), F32(0.0))
        step = moved + vector * step[:, size - 2 : size - 1]
        powers.append(step)
    weights = jnp.concatenate(powers, axis=0)
    left = jnp.concatenate([part.astype(F32) for part in parts3(weights)], axis=0).astype(BF16)

    cols_w = lax.broadcasted_iota(jnp.int32, (size, size), 1)
    coords = jnp.where(cols_w < size - 1, pltpu.roll(upper[...], size - 1, 1), F32(0.0))
    mapping = lax.dot_general(
        coords, lower[...], (((1,), (1,)), ((), ())),
        precision=lax.Precision.HIGHEST, preferred_element_type=F32,
    )
    map_ref[...] = mapping[: size - 1, : size - 1]

    for index in range(pieces):
        fetch(index).wait()
        part = pl.ds(index * width, width)
        product = jnp.dot(left, data[:, part], preferred_element_type=F32)
        future_ref[:, part] = product[:H] + product[H : 2 * H] + product[2 * H :]


def forecast(gram, data):
    size, states = data.shape
    return pl.pallas_call(
        forecast_kernel,
        out_shape=(
            jax.ShapeDtypeStruct((size - 1, size - 1), F32),
            jax.ShapeDtypeStruct((H, states), F32),
        ),
        in_specs=[pl.BlockSpec(memory_space=pltpu.VMEM), pl.BlockSpec(memory_space=pltpu.HBM)],
        out_specs=(pl.BlockSpec(memory_space=pltpu.VMEM), pl.BlockSpec(memory_space=pltpu.VMEM)),
        scratch_shapes=[
            pltpu.VMEM((size, size), F32),
            pltpu.VMEM((size, size), F32),
            pltpu.VMEM((size, size), F32),
            pltpu.VMEM((size, states), BF16),
            pltpu.SemaphoreType.DMA((states // FORECAST_COLUMNS,)),
        ],
        compiler_params=pltpu.CompilerParams(vmem_limit_bytes=40 * 2**20),
    )(gram, data)


def solution(mesh):
    def per_device(window_observations):
        data, gram = exchange(window_observations)
        return forecast(gram, data)

    return jax.shard_map(
        per_device,
        mesh=mesh,
        in_specs=(P("snap", "rows"),),
        out_specs=(P(), P(None, ("rows", "snap"))),
        check_vma=False,
    )
```

```python
import functools

import jax
import jax.numpy as jnp
from jax import lax
from jax.experimental import pallas as pl
from jax.experimental.pallas import tpu as pltpu
from jax.sharding import PartitionSpec as P

H = 8
BLOCK = 32
CHUNKS = 8
EARLY = 3
SIDE = 4
FORECAST_COLUMNS = 2048
MESH = pl.DeviceIdType.MESH
F32, BF16 = jnp.float32, jnp.bfloat16


def parts3(value):
    high = value.astype(BF16)
    rest = value - high.astype(F32)
    middle = rest.astype(BF16)
    low = (rest - middle.astype(F32)).astype(BF16)
    return high, middle, low


def exchange_kernel(x_ref, data_ref, gram_ref, held, total, pair, quarters, slab, laps,
                    near_sem, own_sem, send_sem, recv_sem, out_sem, sum_send, sum_recv):
    me_s, me_r = lax.axis_index("snap"), lax.axis_index("rows")
    y_lo, z = me_s // SIDE, lax.rem(me_s, SIDE)
    y_hi, x, core = me_r // (2 * SIDE), lax.rem(me_r // 2, SIDE), lax.rem(me_r, 2)
    y = 2 * y_hi + y_lo
    block = x_ref.shape[0]
    states = data_ref.shape[1]
    width = states // CHUNKS

    def device(dx=0, dy=0, dz=0, dc=0):
        far_y = lax.rem(y + dy, SIDE)
        far_x, far_z, far_c = lax.rem(x + dx, SIDE), lax.rem(z + dz, SIDE), lax.rem(core + dc, 2)
        return (lax.rem(far_y, 2) * SIDE + far_z, (far_y // 2) * 2 * SIDE + far_x * 2 + far_c)

    neighbours = [
        device(dc=1), device(dx=1), device(dx=3), device(dy=1), device(dy=3), device(dz=1), device(dz=3)
    ]

    def greet(semaphore):
        for neighbour in neighbours:
            pl.semaphore_signal(semaphore, inc=1, device_id=neighbour, device_id_type=MESH)
        pl.semaphore_wait(semaphore, len(neighbours))

    my_rows = pl.ds(pl.multiple_of(me_s * block, block), block)

    def columns(chunk):
        return pl.ds(pl.multiple_of(chunk * width, width), width)

    def own_copy(chunk):
        return pltpu.make_async_copy(
            x_ref.at[:, pl.ds(pl.multiple_of(me_s * states + chunk * width, width), width)],
            held.at[my_rows, columns(chunk)],
            own_sem.at[chunk],
        )

    def send(chunk, offset):
        dy, dz = offset // SIDE, offset % SIDE
        peer = lax.rem(y_lo + dy, 2) * SIDE + lax.rem(z + dz, SIDE)
        return pltpu.make_async_remote_copy(
            src_ref=x_ref.at[:, pl.ds(pl.multiple_of(peer * states + chunk * width, width), width)],
            dst_ref=held.at[my_rows, columns(chunk)],
            send_sem=send_sem.at[chunk, offset],
            recv_sem=recv_sem.at[chunk, offset],
            device_id=(peer, me_r),
            device_id_type=MESH,
        )

    others = range(1, 2 * SIDE)

    def start_chunks(first, last, offsets):
        def start(chunk, carry):
            for offset in offsets:
                send(chunk, offset).start()
            return carry

        lax.fori_loop(first, last, start, 0)

    greet(pltpu.get_barrier_semaphore())
    start_chunks(0, EARLY, (4, 1, 3))
    greet(near_sem.at[0])
    start_chunks(0, EARLY, (2, 5, 7))
    greet(near_sem.at[1])
    start_chunks(0, EARLY, (6,))
    start_chunks(EARLY, CHUNKS, (6, 5, 7, 2, 4, 1, 3))
    greet(near_sem.at[2])

    def start_own(chunk, carry):
        own_copy(chunk).start()
        return carry

    lax.fori_loop(0, CHUNKS, start_own, 0)
    total[...] = jnp.zeros_like(total)

    def out_copy(chunk):
        return pltpu.make_async_copy(held.at[:, columns(chunk)], data_ref.at[:, columns(chunk)], out_sem.at[chunk])

    def use_chunk(chunk, carry):
        own_copy(chunk).wait()
        for offset in others:
            send(chunk, offset).wait_recv()
        out_copy(chunk).start()
        piece = held[:, columns(chunk)]
        half = piece.shape[0] // 2
        dims = (((1,), (1,)), ((), ()))
        top = lax.dot_general(piece[:half], piece, dims, preferred_element_type=F32)
        total[:half] += top[:, :half]
        total[half : 2 * half] += top[:, half:]
        total[2 * half :] += lax.dot_general(piece[half:], piece[half:], dims, preferred_element_type=F32)
        return carry

    lax.fori_loop(0, CHUNKS, use_chunk, 0)

    height = total.shape[0]
    half, share = height // 2, height // (2 * SIDE)
    started = []

    def move(source, target, where):
        index = len(started)
        copy = pltpu.make_async_remote_copy(
            src_ref=source, dst_ref=target, send_sem=sum_send.at[index], recv_sem=sum_recv.at[index],
            device_id=where, device_id_type=MESH,
        )
        copy.start()
        started.append(copy)
        return copy

    def half_of(index):
        return pl.ds(pl.multiple_of(index * half, half), half)

    def share_of(far_x):
        return pl.ds(pl.multiple_of(core * half + far_x * share, share), share)

    eight = [(dx, dc) for dx in (2, 1, 3) for dc in (0, 1)] + [(0, 1)]
    copies = []
    for slot, (dx, dc) in enumerate(eight):
        part = pl.ds(pl.multiple_of(lax.rem(core + dc, 2) * half + lax.rem(x + dx, SIDE) * share, share), share)
        copies.append(move(total.at[part], pair.at[slot], device(dx=dx, dc=dc)))
    mine = total[share_of(x)]
    for slot, copy in reversed(list(enumerate(copies))):
        copy.wait_recv()
        mine = mine + pair[slot]
    slab[...] = mine

    place = y * SIDE + z
    copies = []
    for dy in (2, 1, 3, 0):
        for dz in (2, 1, 3, 0):
            if dy or dz:
                copies.append(move(slab, laps.at[place], device(dy=dy, dz=dz)))
    laps[place] = mine
    for copy in copies:
        copy.wait_recv()
    summed = laps[0]
    for index in range(1, SIDE * SIDE):
        summed = summed + laps[index]
    gram_ref[share_of(x)] = summed

    copies = []
    for dx, dc in eight:
        copies.append(move(gram_ref.at[share_of(x)], gram_ref.at[share_of(x)], device(dx=dx, dc=dc)))
    for copy in copies:
        copy.wait_recv()
    for copy in started:
        copy.wait_send()

    def finish(chunk, carry):
        out_copy(chunk).wait()
        for offset in others:
            send(chunk, offset).wait_send()
        return carry

    lax.fori_loop(0, CHUNKS, finish, 0)


def exchange(x):
    block, length = x.shape
    size, states = 2 * SIDE * block, length // (2 * SIDE)
    height, lanes = 3 * size // 2, size // 2
    share = height // (2 * SIDE)
    dma = pltpu.SemaphoreType.DMA
    moves = 14 + SIDE * SIDE - 1
    return pl.pallas_call(
        exchange_kernel,
        out_shape=(
            jax.ShapeDtypeStruct((size, states), BF16),
            jax.ShapeDtypeStruct((height, lanes), F32),
        ),
        in_specs=[pl.BlockSpec(memory_space=pltpu.HBM)],
        out_specs=(pl.BlockSpec(memory_space=pltpu.HBM), pl.BlockSpec(memory_space=pltpu.VMEM)),
        scratch_shapes=[
            pltpu.VMEM((size, states), BF16),
            pltpu.VMEM((height, lanes), F32),
            pltpu.VMEM((7, share, lanes), F32),
            pltpu.VMEM((SIDE, share, lanes), F32),
            pltpu.VMEM((share, lanes), F32),
            pltpu.VMEM((SIDE * SIDE, share, lanes), F32),
            pltpu.SemaphoreType.REGULAR((3,)),
            dma((CHUNKS,)),
            dma((CHUNKS, 2 * SIDE)),
            dma((CHUNKS, 2 * SIDE)),
            dma((CHUNKS,)),
            dma((moves,)),
            dma((moves,)),
        ],
        compiler_params=pltpu.CompilerParams(
            collective_id=0, has_side_effects=True, vmem_limit_bytes=40 * 2**20
        ),
    )(x)


def factor_block(matrix):
    n = matrix.shape[0]
    rows = lax.broadcasted_iota(jnp.int32, (n, 128), 0)
    lanes = lax.broadcasted_iota(jnp.int32, (n, 128), 1)
    unit = jnp.where((lanes >= n) & (lax.rem(lanes, n) == rows), F32(1.0), F32(0.0))
    whole = unit + jnp.concatenate([matrix, jnp.zeros((n, 128 - n), F32)], axis=1)
    eight = lax.broadcasted_iota(jnp.int32, (8, 128), 0)
    tiles = [whole[k : k + 8] for k in range(0, n, 8)]

    def spread(tile, lane):
        return jnp.broadcast_to(tile[:, lane : lane + 1], (8, 128))

    for now, tile in enumerate(tiles):
        k = 8 * now
        later = range(now + 1, len(tiles))
        row = [jnp.broadcast_to(tile[i : i + 1], (8, 128)) for i in range(8)]
        pivot = [[spread(row[i], k + j) if j >= i else None for j in range(8)] for i in range(8)]
        column = {t: [spread(tiles[t], k + i) for i in range(8)] for t in later}
        inverse = [None] * 8
        scale = None
        for i in range(8):
            if i == 7 and not later:
                break
            near = pltpu.reciprocal(pivot[i][i], approx=True)
            off = pivot[i][i] * near
            exact = near * (F32(2.0) - off)
            exact = exact * (F32(2.0) - pivot[i][i] * exact)
            inverse[i] = exact if scale is None else exact * scale
            scale = off if scale is None else scale * off
            for j in range(i + 1, 8):
                factor = pivot[i][j] * exact
                rough = pivot[i][j] * near
                for m in range(j, 8):
                    pivot[j][m] = off * pivot[j][m] - rough * pivot[i][m]
                row[j] = row[j] - factor * row[i]
                for t in later:
                    column[t][j] = column[t][j] - column[t][i] * factor
        for t in later:
            for i in range(8):
                tiles[t] = tiles[t] - (column[t][i] * inverse[i]) * row[i]
        done = row[0]
        for i in range(1, 8):
            done = jnp.where(eight == i, row[i], done)
        tiles[now] = done
    state = jnp.concatenate(tiles, axis=0)
    diagonal = jnp.sum(jnp.where(rows == lanes, state, F32(0.0)), axis=1, keepdims=True)
    return state, diagonal


def solve(state, lines):
    n = state.shape[0]
    lanes = lax.broadcasted_iota(jnp.int32, state.shape, 1)
    high, middle, low = [part.astype(F32) for part in parts3(state)]
    second = jnp.where(lanes < 3 * n, middle, low)
    left = jnp.concatenate([high, second], axis=1).astype(BF16)
    high, middle, low = parts3(lines)
    none = jnp.zeros_like(high)
    right = jnp.concatenate([none, high, middle, low, none, high, middle, high], axis=0)
    return jnp.dot(left, right, preferred_element_type=F32)


def six_left(value, axis):
    high, middle, low = parts3(value)
    return jnp.concatenate([high, middle, high, low, high, middle], axis=axis)


def six_right(value, axis):
    high, middle, low = parts3(value)
    return jnp.concatenate([high, high, middle, high, low, middle], axis=axis)


def forecast_kernel(gram_ref, data_hbm, map_ref, future_ref, work, upper, lower, data, sems):
    size, states = data.shape
    pieces = sems.shape[0]
    width = states // pieces

    def fetch(index):
        part = pl.ds(index * width, width)
        return pltpu.make_async_copy(data_hbm.at[:, part], data.at[:, part], sems.at[index])

    for index in range(pieces):
        fetch(index).start()

    b = BLOCK
    half = size // 2
    work[:half, :half] = gram_ref[:half]
    work[:half, half:] = gram_ref[half : 2 * half]
    work[half:, half:] = gram_ref[2 * half :]
    work[half:, :half] = jnp.zeros((half, half), F32)
    cols = lax.broadcasted_iota(jnp.int32, (b, size), 1)
    last = None
    for s in range(0, size, b):
        lines = work[s : s + b, :]
        state, diagonal = factor_block(lines[:, s : s + b])
        rows_b = lax.broadcasted_iota(jnp.int32, (b, size), 0)
        inside = (cols >= s) & (cols < s + b)
        lines = jnp.where(inside, jnp.where(cols == rows_b + s, F32(1.0), F32(0.0)), lines)
        solved = solve(state, lines)
        if s + b < size:
            first = 0 if s + b < size // 2 else size // 2
            scaled = jnp.where(cols >= s + b, solved, F32(0.0)) * (F32(1.0) / diagonal)
            update = lax.dot_general(
                six_left(scaled[:, first:], 0), six_right(solved, 0), (((0,), (0,)), ((), ())),
                preferred_element_type=F32,
            )
            kept = work[s + b :, :]
            cols_k = lax.broadcasted_iota(jnp.int32, kept.shape, 1)
            kept = jnp.where((cols_k >= s) & (cols_k < s + b), F32(0.0), kept)
            work[s + b :, :] = kept - update[s + b - first :, :]
        root = lax.rsqrt(diagonal)
        corner = jnp.where(inside, F32(0.0), jnp.where(cols >= s + b, solved, F32(0.0)))
        placed = [state[:, :b]]
        if s:
            placed.insert(0, jnp.zeros((b, s), F32))
        if s + b < size:
            placed.append(jnp.zeros((b, size - s - b), F32))
        diag_rows = jnp.concatenate(placed, axis=1)
        diag_rows = jnp.where(cols >= rows_b + s, diag_rows, F32(0.0))
        upper[s : s + b, :] = (corner + diag_rows) * root
        low_rows = jnp.where(cols < s + b, solved, F32(0.0))
        lower[s : s + b, :] = low_rows * root
        last = low_rows

    cols_1 = lax.broadcasted_iota(jnp.int32, (1, size), 1)
    vector = jnp.where(cols_1 < size - 1, -last[b - 1 : b, :], F32(0.0))
    step, powers = vector, []
    for _ in range(H):
        moved = jnp.where((cols_1 >= 1) & (cols_1 < size - 1), pltpu.roll(step, 1, 1), F32(0.0))
        step = moved + vector * step[:, size - 2 : size - 1]
        powers.append(step)
    weights = jnp.concatenate(powers, axis=0)
    left = jnp.concatenate([part.astype(F32) for part in parts3(weights)], axis=0).astype(BF16)

    cols_w = lax.broadcasted_iota(jnp.int32, (size, size), 1)
    coords = jnp.where(cols_w < size - 1, pltpu.roll(upper[...], size - 1, 1), F32(0.0))
    mapping = lax.dot_general(
        coords, lower[...], (((1,), (1,)), ((), ())),
        precision=lax.Precision.HIGHEST, preferred_element_type=F32,
    )
    map_ref[...] = mapping[: size - 1, : size - 1]

    for index in range(pieces):
        fetch(index).wait()
        part = pl.ds(index * width, width)
        product = jnp.dot(left, data[:, part], preferred_element_type=F32)
        future_ref[:, part] = product[:H] + product[H : 2 * H] + product[2 * H :]


def forecast(gram, data):
    size, states = data.shape
    return pl.pallas_call(
        forecast_kernel,
        out_shape=(
            jax.ShapeDtypeStruct((size - 1, size - 1), F32),
            jax.ShapeDtypeStruct((H, states), F32),
        ),
        in_specs=[pl.BlockSpec(memory_space=pltpu.VMEM), pl.BlockSpec(memory_space=pltpu.HBM)],
        out_specs=(pl.BlockSpec(memory_space=pltpu.VMEM), pl.BlockSpec(memory_space=pltpu.VMEM)),
        scratch_shapes=[
            pltpu.VMEM((size, size), F32),
            pltpu.VMEM((size, size), F32),
            pltpu.VMEM((size, size), F32),
            pltpu.VMEM((size, states), BF16),
            pltpu.SemaphoreType.DMA((states // FORECAST_COLUMNS,)),
        ],
        compiler_params=pltpu.CompilerParams(vmem_limit_bytes=40 * 2**20),
    )(gram, data)


def solution(mesh):
    def per_device(window_observations):
        data, gram = exchange(window_observations)
        return forecast(gram, data)

    return jax.shard_map(
        per_device,
        mesh=mesh,
        in_specs=(P("snap", "rows"),),
        out_specs=(P(), P(None, ("rows", "snap"))),
        check_vma=False,
    )
```

```python
import functools

import jax
import jax.numpy as jnp
from jax import lax
from jax.experimental import pallas as pl
from jax.experimental.pallas import tpu as pltpu
from jax.sharding import PartitionSpec as P

H = 8
BLOCK = 32
CHUNKS = 8
EARLY = 3
SIDE = 4
FORECAST_COLUMNS = 2048
MESH = pl.DeviceIdType.MESH
F32, BF16 = jnp.float32, jnp.bfloat16


def parts3(value):
    high = value.astype(BF16)
    rest = value - high.astype(F32)
    middle = rest.astype(BF16)
    low = (rest - middle.astype(F32)).astype(BF16)
    return high, middle, low


def exchange_kernel(x_ref, data_ref, gram_ref, held, total, packed, pair, slab, laps,
                    near_sem, own_sem, send_sem, recv_sem, out_sem, sum_send, sum_recv):
    me_s, me_r = lax.axis_index("snap"), lax.axis_index("rows")
    y_lo, z = me_s // SIDE, lax.rem(me_s, SIDE)
    y_hi, x, core = me_r // (2 * SIDE), lax.rem(me_r // 2, SIDE), lax.rem(me_r, 2)
    y = 2 * y_hi + y_lo
    block = x_ref.shape[0]
    states = data_ref.shape[1]
    width = states // CHUNKS

    def device(dx=0, dy=0, dz=0, dc=0):
        far_y = lax.rem(y + dy, SIDE)
        far_x, far_z, far_c = lax.rem(x + dx, SIDE), lax.rem(z + dz, SIDE), lax.rem(core + dc, 2)
        return (lax.rem(far_y, 2) * SIDE + far_z, (far_y // 2) * 2 * SIDE + far_x * 2 + far_c)

    neighbours = [
        device(dc=1), device(dx=1), device(dx=3), device(dy=1), device(dy=3), device(dz=1), device(dz=3)
    ]

    def greet(semaphore):
        for neighbour in neighbours:
            pl.semaphore_signal(semaphore, inc=1, device_id=neighbour, device_id_type=MESH)
        pl.semaphore_wait(semaphore, len(neighbours))

    my_rows = pl.ds(pl.multiple_of(me_s * block, block), block)

    def columns(chunk):
        return pl.ds(pl.multiple_of(chunk * width, width), width)

    def own_copy(chunk):
        return pltpu.make_async_copy(
            x_ref.at[:, pl.ds(pl.multiple_of(me_s * states + chunk * width, width), width)],
            held.at[my_rows, columns(chunk)],
            own_sem.at[chunk],
        )

    def send(chunk, offset):
        dy, dz = offset // SIDE, offset % SIDE
        peer = lax.rem(y_lo + dy, 2) * SIDE + lax.rem(z + dz, SIDE)
        return pltpu.make_async_remote_copy(
            src_ref=x_ref.at[:, pl.ds(pl.multiple_of(peer * states + chunk * width, width), width)],
            dst_ref=held.at[my_rows, columns(chunk)],
            send_sem=send_sem.at[chunk, offset],
            recv_sem=recv_sem.at[chunk, offset],
            device_id=(peer, me_r),
            device_id_type=MESH,
        )

    others = range(1, 2 * SIDE)

    def start_chunks(first, last, offsets):
        def start(chunk, carry):
            for offset in offsets:
                send(chunk, offset).start()
            return carry

        lax.fori_loop(first, last, start, 0)

    greet(pltpu.get_barrier_semaphore())
    start_chunks(0, EARLY, (4, 1, 3))
    greet(near_sem.at[0])
    start_chunks(0, EARLY, (2, 5, 7))
    greet(near_sem.at[1])
    start_chunks(0, EARLY, (6,))
    start_chunks(EARLY, CHUNKS, (6, 5, 7, 2, 4, 1, 3))
    greet(near_sem.at[2])

    def start_own(chunk, carry):
        own_copy(chunk).start()
        return carry

    lax.fori_loop(0, CHUNKS, start_own, 0)
    total[...] = jnp.zeros_like(total)

    def out_copy(chunk):
        return pltpu.make_async_copy(held.at[:, columns(chunk)], data_ref.at[:, columns(chunk)], out_sem.at[chunk])

    def use_chunk(chunk, carry):
        own_copy(chunk).wait()
        for offset in others:
            send(chunk, offset).wait_recv()
        out_copy(chunk).start()
        piece = held[:, columns(chunk)]
        half = piece.shape[0] // 2
        dims = (((1,), (1,)), ((), ()))
        top = lax.dot_general(piece[:half], piece, dims, preferred_element_type=F32)
        total[:half] += top[:, :half]
        total[half : 2 * half] += top[:, half:]
        total[2 * half :] += lax.dot_general(piece[half:], piece[half:], dims, preferred_element_type=F32)
        return carry

    lax.fori_loop(0, CHUNKS, use_chunk, 0)

    height = packed.shape[0]
    quarter = height // 5
    packed[:quarter] = total[:quarter]
    packed[quarter : 4 * quarter] = total[2 * quarter : 5 * quarter]
    side = lax.broadcasted_iota(jnp.int32, (quarter, 2 * quarter), 1)
    packed[4 * quarter :] = jnp.where(
        side < quarter, pltpu.roll(total[5 * quarter :], quarter, 1), total[quarter : 2 * quarter]
    )
    half, share = height // 2, height // (2 * SIDE)
    started = []

    def move(source, target, where):
        index = len(started)
        copy = pltpu.make_async_remote_copy(
            src_ref=source, dst_ref=target, send_sem=sum_send.at[index], recv_sem=sum_recv.at[index],
            device_id=where, device_id_type=MESH,
        )
        copy.start()
        started.append(copy)
        return copy

    def half_of(index):
        return pl.ds(pl.multiple_of(index * half, half), half)

    def share_of(far_x):
        return pl.ds(pl.multiple_of(core * half + far_x * share, share), share)

    eight = [(dx, dc) for dx in (2, 1, 3) for dc in (0, 1)] + [(0, 1)]
    copies = []
    for slot, (dx, dc) in enumerate(eight):
        part = pl.ds(pl.multiple_of(lax.rem(core + dc, 2) * half + lax.rem(x + dx, SIDE) * share, share), share)
        copies.append(move(packed.at[part], pair.at[slot], device(dx=dx, dc=dc)))
    mine = packed[share_of(x)]
    for slot, copy in reversed(list(enumerate(copies))):
        copy.wait_recv()
        mine = mine + pair[slot]
    slab[...] = mine

    place = y * SIDE + z
    copies = []
    for dy in (2, 1, 3, 0):
        for dz in (2, 1, 3, 0):
            if dy or dz:
                copies.append(move(slab, laps.at[place], device(dy=dy, dz=dz)))
    laps[place] = mine

    def finish(chunk, carry):
        out_copy(chunk).wait()
        for offset in others:
            send(chunk, offset).wait_send()
        return carry

    lax.fori_loop(0, CHUNKS, finish, 0)

    for copy in started[:7]:
        copy.wait_send()
    for copy in copies:
        copy.wait_recv()
    summed = laps[0]
    for index in range(1, SIDE * SIDE):
        summed = summed + laps[index]
    gram_ref[share_of(x)] = summed

    copies = []
    for dx, dc in eight:
        copies.append(move(gram_ref.at[share_of(x)], gram_ref.at[share_of(x)], device(dx=dx, dc=dc)))
    for copy in started[7 : len(started) - 7]:
        copy.wait_send()
    for copy in copies:
        copy.wait_recv()
    for copy in copies:
        copy.wait_send()


def exchange(x):
    block, length = x.shape
    size, states = 2 * SIDE * block, length // (2 * SIDE)
    height, lanes = 5 * size // 4, size // 2
    share = height // (2 * SIDE)
    dma = pltpu.SemaphoreType.DMA
    moves = 14 + SIDE * SIDE - 1
    return pl.pallas_call(
        exchange_kernel,
        out_shape=(
            jax.ShapeDtypeStruct((size, states), BF16),
            jax.ShapeDtypeStruct((height, lanes), F32),
        ),
        in_specs=[pl.BlockSpec(memory_space=pltpu.HBM)],
        out_specs=(pl.BlockSpec(memory_space=pltpu.HBM), pl.BlockSpec(memory_space=pltpu.VMEM)),
        scratch_shapes=[
            pltpu.VMEM((size, states), BF16),
            pltpu.VMEM((3 * lanes, lanes), F32),
            pltpu.VMEM((height, lanes), F32),
            pltpu.VMEM((7, share, lanes), F32),
            pltpu.VMEM((share, lanes), F32),
            pltpu.VMEM((SIDE * SIDE, share, lanes), F32),
            pltpu.SemaphoreType.REGULAR((3,)),
            dma((CHUNKS,)),
            dma((CHUNKS, 2 * SIDE)),
            dma((CHUNKS, 2 * SIDE)),
            dma((CHUNKS,)),
            dma((moves,)),
            dma((moves,)),
        ],
        compiler_params=pltpu.CompilerParams(
            collective_id=0, has_side_effects=True, vmem_limit_bytes=40 * 2**20
        ),
    )(x)


def factor_block(matrix):
    n = matrix.shape[0]
    rows = lax.broadcasted_iota(jnp.int32, (n, 128), 0)
    lanes = lax.broadcasted_iota(jnp.int32, (n, 128), 1)
    unit = jnp.where((lanes >= n) & (lax.rem(lanes, n) == rows), F32(1.0), F32(0.0))
    whole = unit + jnp.concatenate([matrix, jnp.zeros((n, 128 - n), F32)], axis=1)
    eight = lax.broadcasted_iota(jnp.int32, (8, 128), 0)
    tiles = [whole[k : k + 8] for k in range(0, n, 8)]

    def spread(tile, lane):
        return jnp.broadcast_to(tile[:, lane : lane + 1], (8, 128))

    for now, tile in enumerate(tiles):
        k = 8 * now
        later = range(now + 1, len(tiles))
        row = [jnp.broadcast_to(tile[i : i + 1], (8, 128)) for i in range(8)]
        pivot = [[spread(row[i], k + j) if j >= i else None for j in range(8)] for i in range(8)]
        column = {t: [spread(tiles[t], k + i) for i in range(8)] for t in later}
        inverse = [None] * 8
        scale = None
        for i in range(8):
            if i == 7 and not later:
                break
            near = pltpu.reciprocal(pivot[i][i], approx=True)
            off = pivot[i][i] * near
            exact = near * (F32(2.0) - off)
            exact = exact * (F32(2.0) - pivot[i][i] * exact)
            inverse[i] = exact if scale is None else exact * scale
            scale = off if scale is None else scale * off
            for j in range(i + 1, 8):
                factor = pivot[i][j] * exact
                rough = pivot[i][j] * near
                for m in range(j, 8):
                    pivot[j][m] = off * pivot[j][m] - rough * pivot[i][m]
                row[j] = row[j] - factor * row[i]
                for t in later:
                    column[t][j] = column[t][j] - column[t][i] * factor
        for t in later:
            for i in range(8):
                tiles[t] = tiles[t] - (column[t][i] * inverse[i]) * row[i]
        done = row[0]
        for i in range(1, 8):
            done = jnp.where(eight == i, row[i], done)
        tiles[now] = done
    state = jnp.concatenate(tiles, axis=0)
    diagonal = jnp.sum(jnp.where(rows == lanes, state, F32(0.0)), axis=1, keepdims=True)
    return state, diagonal


def solve(state, lines):
    n = state.shape[0]
    lanes = lax.broadcasted_iota(jnp.int32, state.shape, 1)
    high, middle, low = [part.astype(F32) for part in parts3(state)]
    second = jnp.where(lanes < 3 * n, middle, low)
    left = jnp.concatenate([high, second], axis=1).astype(BF16)
    high, middle, low = parts3(lines)
    none = jnp.zeros_like(high)
    right = jnp.concatenate([none, high, middle, low, none, high, middle, high], axis=0)
    return jnp.dot(left, right, preferred_element_type=F32)


def six_left(value, axis):
    high, middle, low = parts3(value)
    return jnp.concatenate([high, middle, high, low, high, middle], axis=axis)


def six_right(value, axis):
    high, middle, low = parts3(value)
    return jnp.concatenate([high, high, middle, high, low, middle], axis=axis)


def forecast_kernel(gram_ref, data_hbm, map_ref, future_ref, work, upper, lower, data, sems):
    size, states = data.shape
    pieces = sems.shape[0]
    width = states // pieces

    def fetch(index):
        part = pl.ds(index * width, width)
        return pltpu.make_async_copy(data_hbm.at[:, part], data.at[:, part], sems.at[index])

    for index in range(pieces):
        fetch(index).start()

    b = BLOCK
    half = size // 2
    quarter = half // 2
    work[:quarter, :half] = gram_ref[:quarter]
    work[:half, half:] = gram_ref[quarter : 3 * quarter]
    work[half : half + quarter, half:] = gram_ref[3 * quarter : 4 * quarter]
    work[quarter:half, :half] = gram_ref[4 * quarter :]
    work[half + quarter :, half:] = pltpu.roll(gram_ref[4 * quarter :], quarter, 1)
    work[half:, :half] = jnp.zeros((half, half), F32)
    cols = lax.broadcasted_iota(jnp.int32, (b, size), 1)
    last = None
    for s in range(0, size, b):
        lines = work[s : s + b, :]
        state, diagonal = factor_block(lines[:, s : s + b])
        rows_b = lax.broadcasted_iota(jnp.int32, (b, size), 0)
        inside = (cols >= s) & (cols < s + b)
        lines = jnp.where(inside, jnp.where(cols == rows_b + s, F32(1.0), F32(0.0)), lines)
        solved = solve(state, lines)
        if s + b < size:
            first = 0 if s + b < size // 2 else size // 2
            scaled = jnp.where(cols >= s + b, solved, F32(0.0)) * (F32(1.0) / diagonal)
            update = lax.dot_general(
                six_left(scaled[:, first:], 0), six_right(solved, 0), (((0,), (0,)), ((), ())),
                preferred_element_type=F32,
            )
            kept = work[s + b :, :]
            cols_k = lax.broadcasted_iota(jnp.int32, kept.shape, 1)
            kept = jnp.where((cols_k >= s) & (cols_k < s + b), F32(0.0), kept)
            work[s + b :, :] = kept - update[s + b - first :, :]
        root = lax.rsqrt(diagonal)
        corner = jnp.where(inside, F32(0.0), jnp.where(cols >= s + b, solved, F32(0.0)))
        placed = [state[:, :b]]
        if s:
            placed.insert(0, jnp.zeros((b, s), F32))
        if s + b < size:
            placed.append(jnp.zeros((b, size - s - b), F32))
        diag_rows = jnp.concatenate(placed, axis=1)
        diag_rows = jnp.where(cols >= rows_b + s, diag_rows, F32(0.0))
        upper[s : s + b, :] = (corner + diag_rows) * root
        low_rows = jnp.where(cols < s + b, solved, F32(0.0))
        lower[s : s + b, :] = low_rows * root
        last = low_rows

    cols_1 = lax.broadcasted_iota(jnp.int32, (1, size), 1)
    vector = jnp.where(cols_1 < size - 1, -last[b - 1 : b, :], F32(0.0))
    step, powers = vector, []
    for _ in range(H):
        moved = jnp.where((cols_1 >= 1) & (cols_1 < size - 1), pltpu.roll(step, 1, 1), F32(0.0))
        step = moved + vector * step[:, size - 2 : size - 1]
        powers.append(step)
    weights = jnp.concatenate(powers, axis=0)
    left = jnp.concatenate([part.astype(F32) for part in parts3(weights)], axis=0).astype(BF16)

    cols_w = lax.broadcasted_iota(jnp.int32, (size, size), 1)
    coords = jnp.where(cols_w < size - 1, pltpu.roll(upper[...], size - 1, 1), F32(0.0))
    mapping = lax.dot_general(
        coords, lower[...], (((1,), (1,)), ((), ())),
        precision=lax.Precision.HIGHEST, preferred_element_type=F32,
    )
    map_ref[...] = mapping[: size - 1, : size - 1]

    for index in range(pieces):
        fetch(index).wait()
        part = pl.ds(index * width, width)
        product = jnp.dot(left, data[:, part], preferred_element_type=F32)
        future_ref[:, part] = product[:H] + product[H : 2 * H] + product[2 * H :]


def forecast(gram, data):
    size, states = data.shape
    return pl.pallas_call(
        forecast_kernel,
        out_shape=(
            jax.ShapeDtypeStruct((size - 1, size - 1), F32),
            jax.ShapeDtypeStruct((H, states), F32),
        ),
        in_specs=[pl.BlockSpec(memory_space=pltpu.VMEM), pl.BlockSpec(memory_space=pltpu.HBM)],
        out_specs=(pl.BlockSpec(memory_space=pltpu.VMEM), pl.BlockSpec(memory_space=pltpu.VMEM)),
        scratch_shapes=[
            pltpu.VMEM((size, size), F32),
            pltpu.VMEM((size, size), F32),
            pltpu.VMEM((size, size), F32),
            pltpu.VMEM((size, states), BF16),
            pltpu.SemaphoreType.DMA((states // FORECAST_COLUMNS,)),
        ],
        compiler_params=pltpu.CompilerParams(vmem_limit_bytes=40 * 2**20),
    )(gram, data)


def solution(mesh):
    def per_device(window_observations):
        data, gram = exchange(window_observations)
        return forecast(gram, data)

    return jax.shard_map(
        per_device,
        mesh=mesh,
        in_specs=(P("snap", "rows"),),
        out_specs=(P(), P(None, ("rows", "snap"))),
        check_vma=False,
    )
```

```python
import functools

import jax
import jax.numpy as jnp
from jax import lax
from jax.experimental import pallas as pl
from jax.experimental.pallas import tpu as pltpu
from jax.sharding import PartitionSpec as P

H = 8
BLOCK = 32
CHUNKS = 8
EARLY = 3
SIDE = 4
FORECAST_COLUMNS = 8192
MESH = pl.DeviceIdType.MESH
F32, BF16 = jnp.float32, jnp.bfloat16


def parts3(value):
    high = value.astype(BF16)
    rest = value - high.astype(F32)
    middle = rest.astype(BF16)
    low = (rest - middle.astype(F32)).astype(BF16)
    return high, middle, low


def exchange_kernel(x_ref, data_ref, gram_ref, held, total, packed, pair, slab, laps,
                    near_sem, own_sem, send_sem, recv_sem, out_sem, sum_send, sum_recv):
    me_s, me_r = lax.axis_index("snap"), lax.axis_index("rows")
    y_lo, z = me_s // SIDE, lax.rem(me_s, SIDE)
    y_hi, x, core = me_r // (2 * SIDE), lax.rem(me_r // 2, SIDE), lax.rem(me_r, 2)
    y = 2 * y_hi + y_lo
    block = x_ref.shape[0]
    states = data_ref.shape[1]
    width = states // CHUNKS

    def device(dx=0, dy=0, dz=0, dc=0):
        far_y = lax.rem(y + dy, SIDE)
        far_x, far_z, far_c = lax.rem(x + dx, SIDE), lax.rem(z + dz, SIDE), lax.rem(core + dc, 2)
        return (lax.rem(far_y, 2) * SIDE + far_z, (far_y // 2) * 2 * SIDE + far_x * 2 + far_c)

    neighbours = [
        device(dc=1), device(dx=1), device(dx=3), device(dy=1), device(dy=3), device(dz=1), device(dz=3)
    ]

    def greet(semaphore):
        for neighbour in neighbours:
            pl.semaphore_signal(semaphore, inc=1, device_id=neighbour, device_id_type=MESH)
        pl.semaphore_wait(semaphore, len(neighbours))

    my_rows = pl.ds(pl.multiple_of(me_s * block, block), block)

    def columns(chunk):
        return pl.ds(pl.multiple_of(chunk * width, width), width)

    def own_copy(chunk):
        return pltpu.make_async_copy(
            x_ref.at[:, pl.ds(pl.multiple_of(me_s * states + chunk * width, width), width)],
            held.at[my_rows, columns(chunk)],
            own_sem.at[chunk],
        )

    def send(chunk, offset):
        dy, dz = offset // SIDE, offset % SIDE
        peer = lax.rem(y_lo + dy, 2) * SIDE + lax.rem(z + dz, SIDE)
        return pltpu.make_async_remote_copy(
            src_ref=x_ref.at[:, pl.ds(pl.multiple_of(peer * states + chunk * width, width), width)],
            dst_ref=held.at[my_rows, columns(chunk)],
            send_sem=send_sem.at[chunk, offset],
            recv_sem=recv_sem.at[chunk, offset],
            device_id=(peer, me_r),
            device_id_type=MESH,
        )

    others = range(1, 2 * SIDE)

    def start_chunks(first, last, offsets):
        def start(chunk, carry):
            for offset in offsets:
                send(chunk, offset).start()
            return carry

        lax.fori_loop(first, last, start, 0)

    greet(pltpu.get_barrier_semaphore())
    start_chunks(0, EARLY, (4, 1, 3))
    greet(near_sem.at[0])
    start_chunks(0, EARLY, (2, 5, 7))
    greet(near_sem.at[1])
    start_chunks(0, EARLY, (6,))
    start_chunks(EARLY, CHUNKS, (6, 5, 7, 2, 4, 1, 3))
    greet(near_sem.at[2])

    def start_own(chunk, carry):
        own_copy(chunk).start()
        return carry

    lax.fori_loop(0, CHUNKS, start_own, 0)
    total[...] = jnp.zeros_like(total)

    def out_copy(chunk):
        return pltpu.make_async_copy(held.at[:, columns(chunk)], data_ref.at[:, columns(chunk)], out_sem.at[chunk])

    def use_chunk(chunk, carry):
        own_copy(chunk).wait()
        for offset in others:
            send(chunk, offset).wait_recv()
        out_copy(chunk).start()
        piece = held[:, columns(chunk)]
        half = piece.shape[0] // 2
        dims = (((1,), (1,)), ((), ()))
        top = lax.dot_general(piece[:half], piece, dims, preferred_element_type=F32)
        total[:half] += top[:, :half]
        total[half : 2 * half] += top[:, half:]
        total[2 * half :] += lax.dot_general(piece[half:], piece[half:], dims, preferred_element_type=F32)
        return carry

    lax.fori_loop(0, CHUNKS, use_chunk, 0)

    height = packed.shape[0]
    quarter = height // 5
    packed[:quarter] = total[:quarter]
    packed[quarter : 4 * quarter] = total[2 * quarter : 5 * quarter]
    side = lax.broadcasted_iota(jnp.int32, (quarter, 2 * quarter), 1)
    packed[4 * quarter :] = jnp.where(
        side < quarter, pltpu.roll(total[5 * quarter :], quarter, 1), total[quarter : 2 * quarter]
    )
    half, share = height // 2, height // (2 * SIDE)
    started = []

    def move(source, target, where):
        index = len(started)
        copy = pltpu.make_async_remote_copy(
            src_ref=source, dst_ref=target, send_sem=sum_send.at[index], recv_sem=sum_recv.at[index],
            device_id=where, device_id_type=MESH,
        )
        copy.start()
        started.append(copy)
        return copy

    def half_of(index):
        return pl.ds(pl.multiple_of(index * half, half), half)

    def share_of(far_x):
        return pl.ds(pl.multiple_of(core * half + far_x * share, share), share)

    eight = [(dx, dc) for dx in (2, 1, 3) for dc in (0, 1)] + [(0, 1)]
    copies = []
    for slot, (dx, dc) in enumerate(eight):
        part = pl.ds(pl.multiple_of(lax.rem(core + dc, 2) * half + lax.rem(x + dx, SIDE) * share, share), share)
        copies.append(move(packed.at[part], pair.at[slot], device(dx=dx, dc=dc)))
    mine = packed[share_of(x)]
    for slot, copy in reversed(list(enumerate(copies))):
        copy.wait_recv()
        mine = mine + pair[slot]
    slab[...] = mine

    place = y * SIDE + z
    copies = []
    for dy in (2, 1, 3, 0):
        for dz in (2, 1, 3, 0):
            if dy or dz:
                copies.append(move(slab, laps.at[place], device(dy=dy, dz=dz)))
    laps[place] = mine

    def finish(chunk, carry):
        out_copy(chunk).wait()
        for offset in others:
            send(chunk, offset).wait_send()
        return carry

    lax.fori_loop(0, CHUNKS, finish, 0)

    for copy in started[:7]:
        copy.wait_send()
    for copy in copies:
        copy.wait_recv()
    summed = laps[0]
    for index in range(1, SIDE * SIDE):
        summed = summed + laps[index]
    gram_ref[share_of(x)] = summed

    copies = []
    for dx, dc in eight:
        copies.append(move(gram_ref.at[share_of(x)], gram_ref.at[share_of(x)], device(dx=dx, dc=dc)))
    for copy in started[7 : len(started) - 7]:
        copy.wait_send()
    for copy in copies:
        copy.wait_recv()
    for copy in copies:
        copy.wait_send()


def exchange(x):
    block, length = x.shape
    size, states = 2 * SIDE * block, length // (2 * SIDE)
    height, lanes = 5 * size // 4, size // 2
    share = height // (2 * SIDE)
    dma = pltpu.SemaphoreType.DMA
    moves = 14 + SIDE * SIDE - 1
    return pl.pallas_call(
        exchange_kernel,
        out_shape=(
            jax.ShapeDtypeStruct((size, states), BF16),
            jax.ShapeDtypeStruct((height, lanes), F32),
        ),
        in_specs=[pl.BlockSpec(memory_space=pltpu.HBM)],
        out_specs=(pl.BlockSpec(memory_space=pltpu.HBM), pl.BlockSpec(memory_space=pltpu.VMEM)),
        scratch_shapes=[
            pltpu.VMEM((size, states), BF16),
            pltpu.VMEM((3 * lanes, lanes), F32),
            pltpu.VMEM((height, lanes), F32),
            pltpu.VMEM((7, share, lanes), F32),
            pltpu.VMEM((share, lanes), F32),
            pltpu.VMEM((SIDE * SIDE, share, lanes), F32),
            pltpu.SemaphoreType.REGULAR((3,)),
            dma((CHUNKS,)),
            dma((CHUNKS, 2 * SIDE)),
            dma((CHUNKS, 2 * SIDE)),
            dma((CHUNKS,)),
            dma((moves,)),
            dma((moves,)),
        ],
        compiler_params=pltpu.CompilerParams(
            collective_id=0, has_side_effects=True, vmem_limit_bytes=40 * 2**20
        ),
    )(x)


def factor_block(matrix):
    n = matrix.shape[0]
    rows = lax.broadcasted_iota(jnp.int32, (n, 128), 0)
    lanes = lax.broadcasted_iota(jnp.int32, (n, 128), 1)
    unit = jnp.where((lanes >= n) & (lax.rem(lanes, n) == rows), F32(1.0), F32(0.0))
    whole = unit + jnp.concatenate([matrix, jnp.zeros((n, 128 - n), F32)], axis=1)
    eight = lax.broadcasted_iota(jnp.int32, (8, 128), 0)
    tiles = [whole[k : k + 8] for k in range(0, n, 8)]

    def spread(tile, lane):
        return jnp.broadcast_to(tile[:, lane : lane + 1], (8, 128))

    for now, tile in enumerate(tiles):
        k = 8 * now
        later = range(now + 1, len(tiles))
        row = [jnp.broadcast_to(tile[i : i + 1], (8, 128)) for i in range(8)]
        pivot = [[spread(row[i], k + j) if j >= i else None for j in range(8)] for i in range(8)]
        column = {t: [spread(tiles[t], k + i) for i in range(8)] for t in later}
        inverse = [None] * 8
        scale = None
        for i in range(8):
            if i == 7 and not later:
                break
            near = pltpu.reciprocal(pivot[i][i], approx=True)
            off = pivot[i][i] * near
            exact = near * (F32(2.0) - off)
            exact = exact * (F32(2.0) - pivot[i][i] * exact)
            inverse[i] = exact if scale is None else exact * scale
            scale = off if scale is None else scale * off
            for j in range(i + 1, 8):
                factor = pivot[i][j] * exact
                rough = pivot[i][j] * near
                for m in range(j, 8):
                    pivot[j][m] = off * pivot[j][m] - rough * pivot[i][m]
                row[j] = row[j] - factor * row[i]
                for t in later:
                    column[t][j] = column[t][j] - column[t][i] * factor
        for t in later:
            for i in range(8):
                tiles[t] = tiles[t] - (column[t][i] * inverse[i]) * row[i]
        done = row[0]
        for i in range(1, 8):
            done = jnp.where(eight == i, row[i], done)
        tiles[now] = done
    state = jnp.concatenate(tiles, axis=0)
    diagonal = jnp.sum(jnp.where(rows == lanes, state, F32(0.0)), axis=1, keepdims=True)
    return state, diagonal


def solve(state, lines):
    n = state.shape[0]
    lanes = lax.broadcasted_iota(jnp.int32, state.shape, 1)
    high, middle, low = [part.astype(F32) for part in parts3(state)]
    second = jnp.where(lanes < 3 * n, middle, low)
    left = jnp.concatenate([high, second], axis=1).astype(BF16)
    high, middle, low = parts3(lines)
    none = jnp.zeros_like(high)
    right = jnp.concatenate([none, high, middle, low, none, high, middle, high], axis=0)
    return jnp.dot(left, right, preferred_element_type=F32)


def six_left(value, axis):
    high, middle, low = parts3(value)
    return jnp.concatenate([high, middle, high, low, high, middle], axis=axis)


def six_right(value, axis):
    high, middle, low = parts3(value)
    return jnp.concatenate([high, high, middle, high, low, middle], axis=axis)


def forecast_kernel(gram_ref, data_hbm, map_ref, future_ref, work, upper, lower, data, sems):
    size, states = data.shape
    pieces = sems.shape[0]
    width = states // pieces

    def fetch(index):
        part = pl.ds(index * width, width)
        return pltpu.make_async_copy(data_hbm.at[:, part], data.at[:, part], sems.at[index])

    for index in range(pieces):
        fetch(index).start()

    b = BLOCK
    half = size // 2
    quarter = half // 2
    work[:quarter, :half] = gram_ref[:quarter]
    work[:half, half:] = gram_ref[quarter : 3 * quarter]
    work[half : half + quarter, half:] = gram_ref[3 * quarter : 4 * quarter]
    work[quarter:half, :half] = gram_ref[4 * quarter :]
    work[half + quarter :, half:] = pltpu.roll(gram_ref[4 * quarter :], quarter, 1)
    work[half:, :half] = jnp.zeros((half, half), F32)
    cols = lax.broadcasted_iota(jnp.int32, (b, size), 1)
    last = None
    for s in range(0, size, b):
        lines = work[s : s + b, :]
        state, diagonal = factor_block(lines[:, s : s + b])
        rows_b = lax.broadcasted_iota(jnp.int32, (b, size), 0)
        inside = (cols >= s) & (cols < s + b)
        lines = jnp.where(inside, jnp.where(cols == rows_b + s, F32(1.0), F32(0.0)), lines)
        solved = solve(state, lines)
        if s + b < size:
            first = 0 if s + b < size // 2 else size // 2
            scaled = jnp.where(cols >= s + b, solved, F32(0.0)) * (F32(1.0) / diagonal)
            update = lax.dot_general(
                six_left(scaled[:, first:], 0), six_right(solved, 0), (((0,), (0,)), ((), ())),
                preferred_element_type=F32,
            )
            kept = work[s + b :, :]
            cols_k = lax.broadcasted_iota(jnp.int32, kept.shape, 1)
            kept = jnp.where((cols_k >= s) & (cols_k < s + b), F32(0.0), kept)
            work[s + b :, :] = kept - update[s + b - first :, :]
        root = lax.rsqrt(diagonal)
        corner = jnp.where(inside, F32(0.0), jnp.where(cols >= s + b, solved, F32(0.0)))
        placed = [state[:, :b]]
        if s:
            placed.insert(0, jnp.zeros((b, s), F32))
        if s + b < size:
            placed.append(jnp.zeros((b, size - s - b), F32))
        diag_rows = jnp.concatenate(placed, axis=1)
        diag_rows = jnp.where(cols >= rows_b + s, diag_rows, F32(0.0))
        upper[s : s + b, :] = (corner + diag_rows) * root
        low_rows = jnp.where(cols < s + b, solved, F32(0.0))
        lower[s : s + b, :] = low_rows * root
        last = low_rows

    cols_1 = lax.broadcasted_iota(jnp.int32, (1, size), 1)
    vector = jnp.where(cols_1 < size - 1, -last[b - 1 : b, :], F32(0.0))
    step, powers = vector, []
    for _ in range(H):
        moved = jnp.where((cols_1 >= 1) & (cols_1 < size - 1), pltpu.roll(step, 1, 1), F32(0.0))
        step = moved + vector * step[:, size - 2 : size - 1]
        powers.append(step)
    weights = jnp.concatenate(powers, axis=0)
    left = jnp.concatenate([part.astype(F32) for part in parts3(weights)], axis=0).astype(BF16)

    cols_w = lax.broadcasted_iota(jnp.int32, (size, size), 1)
    coords = jnp.where(cols_w < size - 1, pltpu.roll(upper[...], size - 1, 1), F32(0.0))
    mapping = lax.dot_general(
        coords, lower[...], (((1,), (1,)), ((), ())),
        precision=lax.Precision.HIGHEST, preferred_element_type=F32,
    )
    map_ref[...] = mapping[: size - 1, : size - 1]

    for index in range(pieces):
        fetch(index).wait()
        part = pl.ds(index * width, width)
        product = jnp.dot(left, data[:, part], preferred_element_type=F32)
        future_ref[:, part] = product[:H] + product[H : 2 * H] + product[2 * H :]


def forecast(gram, data):
    size, states = data.shape
    return pl.pallas_call(
        forecast_kernel,
        out_shape=(
            jax.ShapeDtypeStruct((size - 1, size - 1), F32),
            jax.ShapeDtypeStruct((H, states), F32),
        ),
        in_specs=[pl.BlockSpec(memory_space=pltpu.VMEM), pl.BlockSpec(memory_space=pltpu.HBM)],
        out_specs=(pl.BlockSpec(memory_space=pltpu.VMEM), pl.BlockSpec(memory_space=pltpu.VMEM)),
        scratch_shapes=[
            pltpu.VMEM((size, size), F32),
            pltpu.VMEM((size, size), F32),
            pltpu.VMEM((size, size), F32),
            pltpu.VMEM((size, states), BF16),
            pltpu.SemaphoreType.DMA((states // FORECAST_COLUMNS,)),
        ],
        compiler_params=pltpu.CompilerParams(vmem_limit_bytes=40 * 2**20),
    )(gram, data)


def solution(mesh):
    def per_device(window_observations):
        data, gram = exchange(window_observations)
        return forecast(gram, data)

    return jax.shard_map(
        per_device,
        mesh=mesh,
        in_specs=(P("snap", "rows"),),
        out_specs=(P(), P(None, ("rows", "snap"))),
        check_vma=False,
    )
```
